32 devices in a mesh: groups: 2 (over y), tm: 4 (over z), dp: 2 (over x), state: 2 (over core).
Axes of the slice: x: 2, y: 2, z: 4, core: 2. Of those that a mesh axis runs over, the one named last changes fastest.
Arguments:
- frames: bfloat16 [4, 1024, 256], P(('groups', 'dp'), ('tm', 'state')), parts along dimension 0, may hold values from -6 to 6
- first_layer_weight: bfloat16 [3, 256, 128], replicated, may hold values from -0.21875 to 0.21875
- second_layer_weight: bfloat16 [3, 128, 128], replicated, may hold values from -0.3125 to 0.3125
- readout: float32 [256, 256], replicated, may hold values from -0.375 to 0.375
- obs_gain: float32 [256, 128], replicated, may hold values from -1 to 1
- transition: float32 [256, 256], replicated, may hold values from -1 to 1
- smoother_gain: float32 [256, 256], replicated, may hold values from -1 to 1
- smooth_blend: float32 [256, 256], replicated, may hold values from -1 to 1
Outputs:
- smoothed: float32 [4, 1024, 256], P(('groups', 'dp'), ('tm', 'state')), parts along dimension 0
- grad_first: float32 [6, 256, 128], P('groups'), parts along dimension 0
- grad_second: float32 [6, 128, 128], P('groups'), parts along dimension 0
- grad_readout: float32 [512, 256], P('groups'), parts along dimension 0
- loss: float32 [2], P('groups'), parts along dimension 0
The draws below stay inside these ranges and needn't reach their ends.
There are 2 independent parts, one for each index of `groups`. The reference program is written for one: setup_inputs(seed, part) draws one part's arguments, and reference() takes and returns one part's arrays. A program takes and returns all parts, laid end to end along the dimension named above; an argument that names none is the same for every part. Nothing has to cross between parts.
All inputs are finite; a program needn't handle non-finite values.
Results may differ from the reference program's by a relative error of at most 0.0028.
Values may be sent and summed in bfloat16 or wider, within the bound.
A program may use at most 128 MiB of HBM per device.

```python
import math
import jax
import jax.numpy as jnp
from jax import lax

SENS = 256
CH = 128
STATE = 256
KERNEL_TAPS = 3
FIRST_SPACING = 8
SECOND_SPACING = 64
FRAMES = 1024
WINDOWS = 2


def chain_rates(key, salt):
    base = jax.random.fold_in(key, salt)
    key_order, key_fast, key_slow = jax.random.split(base, 3)
    order = jax.random.permutation(key_order, STATE)
    fast = (order < STATE // 2).astype(jnp.float32)
    tau_fast = jnp.exp(jax.random.uniform(key_fast, (STATE,), jnp.float32, math.log(8.0), math.log(50.0)))
    tau_slow = jnp.exp(jax.random.uniform(key_slow, (STATE,), jnp.float32, math.log(FRAMES * 0.5), math.log(FRAMES * 4.0)))
    tau = fast * tau_fast + (1.0 - fast) * tau_slow
    return (jnp.exp(-1.0 / tau), fast)


def rotation(key, salt):
    base = jax.random.fold_in(key, salt)
    key_perm, key_sign = jax.random.split(base, 2)
    column_freq = jax.random.permutation(key_perm, STATE).astype(jnp.float32)
    sign_bits = jax.random.randint(key_sign, (STATE,), 0, 2)
    signs = (2 * sign_bits - 1).astype(jnp.float32)
    row_pos = jnp.arange(STATE).astype(jnp.float32)
    angles = math.pi / STATE * (row_pos[:, None] + 0.5) * column_freq[None, :]
    norms = jnp.where(column_freq == 0.0, math.sqrt(1.0 / STATE), math.sqrt(2.0 / STATE)).astype(jnp.float32)
    return jnp.cos(angles) * (norms * signs)[None, :]


def coupled(key, salt, rates, fast):
    noise = jnp.clip(jax.random.normal(jax.random.fold_in(key, salt), (STATE, STATE), jnp.float32), -4.0, 4.0)
    coupling = noise * (1.0 / math.sqrt(STATE)) * (1.0 - rates)[:, None] * fast[:, None] * (1.0 - fast)[None, :]
    return jnp.diag(rates) + coupling


def rotated(basis, inner):
    turned = jnp.dot(jnp.dot(basis, inner, precision=lax.Precision.HIGHEST), basis.T, precision=lax.Precision.HIGHEST)
    return jnp.clip(turned, -1.0, 1.0)


def draw_transition(key, part):
    rates, fast = chain_rates(key, 11)
    return rotated(rotation(key, 13), coupled(key, 12, rates, fast))


def draw_smoother_gain(key, part):
    rates, fast = chain_rates(key, 21)
    return rotated(rotation(key, 23), coupled(key, 22, rates, fast))


def draw_obs_gain(key, part):
    rates, fast = chain_rates(key, 11)
    noise = jnp.clip(jax.random.normal(jax.random.fold_in(key, 31), (STATE, CH), jnp.float32), -4.0, 4.0)
    inner = noise * jnp.sqrt(1.0 - rates * rates)[:, None] * (1.0 / math.sqrt(CH))
    return jnp.clip(jnp.dot(rotation(key, 13), inner, precision=lax.Precision.HIGHEST), -1.0, 1.0)


def draw_smooth_blend(key, part):
    rates, fast = chain_rates(key, 21)
    factor = jax.random.uniform(jax.random.fold_in(key, 41), (STATE,), jnp.float32, 0.5, 1.5)
    return rotated(rotation(key, 23), jnp.diag((1.0 - rates) * factor))


def block_levels(rng, extent, shards, smallest, largest):
    level = 1.0
    for position, parts in shards:
        heights = jax.random.uniform(jax.random.fold_in(jax.random.fold_in(rng, 6), position), (parts,), jnp.float32, smallest / len(shards), largest / len(shards))
        level = level * jnp.repeat(jnp.exp(heights), extent[position] // parts).reshape((-1,) + (1,) * (len(extent) - 1 - position))
    return level


def gaussian(stream_key, dims, width, reach, shards=(), held_as=jnp.bfloat16):
    array = width * jax.random.normal(stream_key, dims, jnp.float32)
    if shards:
        array = array * block_levels(stream_key, dims, shards, -0.22, 0.18)
    return jnp.clip(array, -reach, reach).astype(held_as)


def setup_inputs(seed: int = 0, part: int = 0) -> dict:
    splits = jax.random.split(jax.random.key(seed), 9)
    part_splits = jax.random.split(jax.random.fold_in(splits[8], part), 9)
    frames = gaussian(part_splits[0], (WINDOWS, FRAMES, SENS), 1.0, 6.0, ((0, 2), (1, 8)))
    first_layer_weight = gaussian(splits[1], (KERNEL_TAPS, SENS, CH), (KERNEL_TAPS * SENS) ** -0.5, 0.21875)
    second_layer_weight = gaussian(splits[2], (KERNEL_TAPS, CH, CH), (KERNEL_TAPS * CH) ** -0.5, 0.3125)
    readout = gaussian(splits[3], (SENS, STATE), STATE ** -0.5, 0.375, (), jnp.float32)
    obs_gain = draw_obs_gain(jax.random.fold_in(splits[8], 71), part)
    transition = draw_transition(jax.random.fold_in(splits[8], 71), part)
    smoother_gain = draw_smoother_gain(jax.random.fold_in(splits[8], 71), part)
    smooth_blend = draw_smooth_blend(jax.random.fold_in(splits[8], 71), part)
    return dict(frames=frames, first_layer_weight=first_layer_weight, second_layer_weight=second_layer_weight, readout=readout, obs_gain=obs_gain, transition=transition, smoother_gain=smoother_gain, smooth_blend=smooth_blend)


HIGHEST = lax.Precision.HIGHEST

def recur(drive_rows, matrix, backward):

    def advance(carried, entry_row):
        updated = jnp.dot(carried, matrix, precision=HIGHEST) + entry_row
        return (updated, updated)
    _, outputs = lax.scan(advance, jnp.zeros((drive_rows.shape[1],), jnp.float32), drive_rows, reverse=backward)
    return outputs

def spaced_taps(padded, weight, gap, frame_length):
    total = jnp.dot(padded[0:frame_length], weight[0], preferred_element_type=jnp.float32)
    for tap_index in range(1, KERNEL_TAPS):
        start_row = tap_index * gap
        total = total + jnp.dot(padded[start_row:start_row + frame_length], weight[tap_index], preferred_element_type=jnp.float32)
    return total

def spaced_taps_backward(padded, weight, gap, frame_length):
    total = jnp.zeros((frame_length, weight.shape[1]), jnp.float32)
    for tap_index in range(KERNEL_TAPS):
        start_row = (KERNEL_TAPS - 1 - tap_index) * gap
        total = total + jnp.dot(padded[start_row:start_row + frame_length], weight[tap_index].T, preferred_element_type=jnp.float32)
    return total

def weight_gradient_pair(padded, cotangent, gap, frame_length):
    return jnp.stack([jnp.dot(padded[tap_index * gap:tap_index * gap + frame_length].T, cotangent, preferred_element_type=jnp.float32) for tap_index in range(KERNEL_TAPS)])

def reference(frames, first_layer_weight, second_layer_weight, readout, obs_gain, transition, smoother_gain, smooth_blend):
    frame_length = FRAMES
    first_receptive_span = KERNEL_TAPS // 2 * FIRST_SPACING
    second_receptive_span = KERNEL_TAPS // 2 * SECOND_SPACING
    scale = 1.0 / (WINDOWS * FRAMES)
    is_last = (jnp.arange(frame_length) == frame_length - 1)[:, None]

    def window_step(signal):
        input_padded = jnp.pad(signal, ((first_receptive_span, first_receptive_span), (0, 0)))
        preactivation = spaced_taps(input_padded, first_layer_weight, FIRST_SPACING, frame_length)
        hidden = jax.nn.gelu(preactivation).astype(jnp.bfloat16)
        middle_padded = jnp.pad(hidden, ((second_receptive_span, second_receptive_span), (0, 0)))
        encoded_frames = spaced_taps(middle_padded, second_layer_weight, SECOND_SPACING, frame_length)
        drive_rows = jnp.dot(encoded_frames, obs_gain.T, precision=HIGHEST)
        filtered = recur(drive_rows, transition.T, False)
        blended = jnp.where(is_last, filtered, jnp.dot(filtered, smooth_blend.T, precision=HIGHEST))
        smoothed = recur(blended, smoother_gain.T, True)
        miss = jnp.dot(smoothed, readout.T, precision=HIGHEST) - signal.astype(jnp.float32)
        d_miss = miss * scale
        grad_read = jnp.dot(d_miss.T, smoothed, precision=HIGHEST)
        adj_smooth = recur(jnp.dot(d_miss, readout, precision=HIGHEST), smoother_gain, False)
        d_filtered = jnp.where(is_last, adj_smooth, jnp.dot(adj_smooth, smooth_blend, precision=HIGHEST))
        adj_filter = recur(d_filtered, transition, True)
        observed_gradient = jnp.dot(adj_filter, obs_gain, precision=HIGHEST).astype(jnp.bfloat16)
        backward_padded = jnp.pad(observed_gradient, ((second_receptive_span, second_receptive_span), (0, 0)))
        hidden_gradient = spaced_taps_backward(backward_padded, second_layer_weight, SECOND_SPACING, frame_length)
        _, gelu_back = jax.vjp(jax.nn.gelu, preactivation)
        preactivation_gradient = gelu_back(hidden_gradient)[0].astype(jnp.bfloat16)
        second_layer_gradient = weight_gradient_pair(middle_padded, observed_gradient, SECOND_SPACING, frame_length)
        first_layer_gradient = weight_gradient_pair(input_padded, preactivation_gradient, FIRST_SPACING, frame_length)
        loss_part = 0.5 * jnp.sum(miss * miss) * scale / SENS
        return (smoothed, first_layer_gradient, second_layer_gradient, grad_read, loss_part)
    smoothed, first_layer_gradient, second_layer_gradient, grad_read, loss_part = lax.map(window_step, frames)
    return (smoothed, lax.optimization_barrier(jnp.sum(first_layer_gradient, axis=0)), lax.optimization_barrier(jnp.sum(second_layer_gradient, axis=0)), lax.optimization_barrier(jnp.sum(grad_read, axis=0)), jnp.sum(loss_part).reshape(1))
```

```python
import functools
import math

import jax
import jax.numpy as jnp
from jax import lax
from jax.experimental import pallas as pl
from jax.experimental.pallas import tpu as pltpu
from jax.sharding import PartitionSpec as P

KERNEL_TAPS = 3
FIRST_SPACING = 8
SECOND_SPACING = 64
EDGE = 80
AXES = ("state", "dp", "tm")
SHORT, WIDE = (jnp.bfloat16, jnp.float32)


def split(array):
    high = array.astype(SHORT)
    return high, (array - high.astype(WIDE)).astype(SHORT)


def dot(a, b, contract):
    return lax.dot_general(a, b, (contract, ((), ())), preferred_element_type=WIDE)


def product(a, b, turned=False):
    contract = ((1,), (1 if turned else 0,))
    return dot(a[0], b[0], contract) + (dot(a[0], b[1], contract) + dot(a[1], b[0], contract))


def square(matrix):
    high = matrix.astype(SHORT)
    left = matrix - high.astype(WIDE)
    middle = left.astype(SHORT)
    low = (left - middle.astype(WIDE)).astype(SHORT)
    contract = ((1,), (0,))
    small = dot(high, low, contract) + dot(low, high, contract) + dot(middle, middle, contract)
    cross = dot(high, middle, contract) + dot(middle, high, contract)
    return dot(high, high, contract) + (cross + small)


def inner(a, b):
    contract = ((0,), (0,))
    return dot(a[0], b[0], contract) + (dot(a[0], b[1], contract) + dot(a[1], b[0], contract))


def remote(src, dst, send_sem, recv_sem, device):
    return pltpu.make_async_remote_copy(
        src_ref=src,
        dst_ref=dst,
        send_sem=send_sem,
        recv_sem=recv_sem,
        device_id=device,
        device_id_type=pl.DeviceIdType.MESH,
    )


class Reduction:
    def __init__(self, rows, sizes, refs):
        (self.total, self.full), self.sends, self.slots = refs[:2], refs[2:5], refs[5:8]
        self.held, (self.send_sem, self.recv_sem) = refs[8:10], refs[10:12]
        self.held = (self.total,) + tuple(self.held)
        self.sizes, self.pending = sizes, []
        self.at = [lax.axis_index(axis) for axis in AXES]
        self.piece = []
        for size in sizes:
            rows //= size
            self.piece.append(rows)

    def region(self, level, index):
        offset = index * self.piece[level]
        for above in range(level):
            offset = offset + self.at[above] * self.piece[above]
        return pl.ds(pl.multiple_of(offset, 16), self.piece[level])

    def start_scatter(self, level):
        self.sends[level][...] = self.held[level][...].astype(SHORT)
        for step in range(1, self.sizes[level]):
            to = lax.rem(self.at[level] + step, self.sizes[level])
            start = pl.multiple_of(to * self.piece[level], 16)
            copy = remote(
                self.sends[level].at[pl.ds(start, self.piece[level])],
                self.slots[level].at[step - 1],
                self.send_sem.at[level, step - 1],
                self.recv_sem.at[level, step - 1],
                {AXES[level]: to},
            )
            copy.start()
            self.pending.append(copy)

    def finish_scatter(self, level):
        for copy in self.pending[-(self.sizes[level] - 1) :]:
            copy.wait_recv()
        start = pl.multiple_of(self.at[level] * self.piece[level], 16)
        value = self.held[level][pl.ds(start, self.piece[level])]
        for step in range(1, self.sizes[level]):
            value = value + self.slots[level][step - 1].astype(WIDE)
        if level + 1 < len(AXES):
            self.held[level + 1][...] = value
        else:
            self.full[self.region(level, self.at[level])] = value.astype(self.full.dtype)

    def start_gather(self, level):
        mine = self.full.at[self.region(level, self.at[level])]
        for step in range(1, self.sizes[level]):
            to = lax.rem(self.at[level] + step, self.sizes[level])
            copy = remote(
                mine,
                mine,
                self.send_sem.at[3 + level, step - 1],
                self.recv_sem.at[3 + level, step - 1],
                {AXES[level]: to},
            )
            copy.start()
            self.pending.append(copy)

    def finish_gather(self, level):
        for step in range(1, self.sizes[level]):
            size = self.sizes[level]
            source = lax.rem(self.at[level] + size - step, size)
            theirs = self.full.at[self.region(level, source)]
            remote(
                theirs,
                theirs,
                self.send_sem.at[3 + level, step - 1],
                self.recv_sem.at[3 + level, step - 1],
                {AXES[level]: source},
            ).wait_recv()

    def drain(self):
        for copy in self.pending:
            copy.wait_send()


def kernel(dims, *refs):
    blocks, cores, sizes, windows, frames_total, levels = dims
    (frames_ref, first_ref, second_ref, readout_ref, gain_ref) = refs[:5]
    (transition_ref, smoother_ref, blend_ref) = refs[5:8]
    (smoothed_out, first_out, second_out, read_out, loss_out) = refs[8:13]
    (ext, power_high, power_low, ends, arrivals, slope) = refs[13:19]
    (halo_send, halo_recv, carry_send, carry_recv) = refs[19:23]
    (loss_send, loss_slots, loss_send_sem, loss_recv_sem) = refs[23:27]
    refs_a, refs_b = refs[27:39], refs[39:51]
    frame_length = frames_ref.shape[1]
    state = transition_ref.shape[0]
    local_levels = frame_length.bit_length() - 1
    place = lax.axis_index("tm") * cores + lax.axis_index("state")
    first_block, last_block = place == 0, place == blocks - 1

    def device(at):
        return {"tm": at // cores, "state": lax.rem(at, cores)}

    ext[...] = jnp.zeros_like(ext)
    arrivals[...] = jnp.zeros_like(arrivals)
    ext[EDGE : EDGE + frame_length] = frames_ref[0]
    barrier = pltpu.get_barrier_semaphore()
    for step in range(1, blocks):
        pl.semaphore_signal(
            barrier,
            inc=1,
            device_id=device(lax.rem(place + step, blocks)),
            device_id_type=pl.DeviceIdType.MESH,
        )
    for step in range(1, sizes[1]):
        pl.semaphore_signal(
            barrier,
            inc=1,
            device_id={"dp": lax.rem(lax.axis_index("dp") + step, sizes[1])},
            device_id_type=pl.DeviceIdType.MESH,
        )
    pl.semaphore_wait(barrier, blocks - 1 + sizes[1] - 1)

    def to_next():
        return remote(
            frames_ref.at[0, frame_length - EDGE : frame_length],
            ext.at[0:EDGE],
            halo_send.at[0],
            halo_recv.at[0],
            device(lax.rem(place + 1, blocks)),
        )

    def to_previous():
        return remote(
            frames_ref.at[0, 0:EDGE],
            ext.at[EDGE + frame_length : 2 * EDGE + frame_length],
            halo_send.at[1],
            halo_recv.at[1],
            device(lax.rem(place + blocks - 1, blocks)),
        )

    @pl.when(jnp.logical_not(last_block))
    def _():
        to_next().start()

    @pl.when(jnp.logical_not(first_block))
    def _():
        to_previous().start()

    def power(which, level):
        return power_high[which, level], power_low[which, level]

    for which, ref in enumerate((transition_ref, smoother_ref)):
        held = ref[...]
        for level in range(levels):
            power_high[which, level], power_low[which, level] = split(held)
            if level + 1 < levels:
                held = square(held)

    gain, readout, blend = [split(ref[...]) for ref in (gain_ref, readout_ref, blend_ref)]

    @pl.when(jnp.logical_not(first_block))
    def _():
        to_next().wait_recv()

    @pl.when(jnp.logical_not(last_block))
    def _():
        to_previous().wait_recv()

    reach = frame_length + 2 * SECOND_SPACING
    low = EDGE - SECOND_SPACING
    taps = jnp.concatenate([first_ref[tap] for tap in range(KERNEL_TAPS)], axis=1)
    partial = dot(ext[...], taps, ((1,), (0,)))
    channels = second_ref.shape[2]
    preact = sum(
        partial[
            low + (tap - 1) * FIRST_SPACING : low + (tap - 1) * FIRST_SPACING + reach,
            tap * channels : (tap + 1) * channels,
        ]
        for tap in range(KERNEL_TAPS)
    )
    where_row = lax.broadcasted_iota(jnp.int32, (reach, channels), 0)
    begin = jnp.where(first_block, SECOND_SPACING, 0)
    end = jnp.where(last_block, SECOND_SPACING + frame_length, reach)
    inside = jnp.logical_and(where_row >= begin, where_row < end)
    root = math.sqrt(2.0 / math.pi)
    squared = preact * preact
    bent = jnp.tanh(root * (preact + 0.044715 * (squared * preact)))
    half = 0.5 * (1.0 + bent)
    hidden = jnp.where(inside, preact * half, 0.0).astype(SHORT)
    bend = 0.5 * preact * (1.0 - bent * bent) * (root * (1.0 + 3 * 0.044715 * squared))
    slope[...] = jnp.where(inside, half + bend, 0.0)
    spaced = jnp.concatenate(
        [
            hidden[tap * SECOND_SPACING : tap * SECOND_SPACING + frame_length]
            for tap in range(KERNEL_TAPS)
        ],
        axis=1,
    )
    second = jnp.concatenate([second_ref[tap] for tap in range(KERNEL_TAPS)], axis=0)
    observed = dot(spaced, second, ((1,), (0,)))
    drive = product(split(observed), gain, True)

    row = lax.broadcasted_iota(jnp.int32, (frame_length, state), 0)
    row8 = lax.broadcasted_iota(jnp.int32, (8, state), 0)

    def local_scan(running, which, turned, reverse):
        for level in range(local_levels):
            stride = 1 << level
            matrix = power(which, level)
            if stride < 8:
                moved = pltpu.roll(running, frame_length - stride if reverse else stride, 0)
                kept = row < frame_length - stride if reverse else row >= stride
                moved = jnp.where(kept, moved, 0.0)
                running = running + product(split(moved), matrix, turned)
            elif reverse:
                added = product(split(running[stride:]), matrix, turned)
                running = jnp.concatenate(
                    [running[: frame_length - stride] + added, running[frame_length - stride :]]
                )
            else:
                added = product(split(running[: frame_length - stride]), matrix, turned)
                running = jnp.concatenate([running[:stride], running[stride:] + added])
        return running

    def carry_copy(index, step, reverse):
        to = lax.rem(place + (blocks - step if reverse else step), blocks)
        return remote(
            ends.at[index],
            arrivals.at[index, step - 1],
            carry_send.at[index, step - 1],
            carry_recv.at[index, step - 1],
            device(to),
        )

    def has_later(step, reverse):
        return place >= step if reverse else place + step < blocks

    def start_carry(index, running, reverse):
        ends[index] = running[0:1] if reverse else running[frame_length - 1 :]
        for step in range(1, blocks):

            @pl.when(has_later(step, reverse))
            def _():
                carry_copy(index, step, reverse).start()

    def finish_carry(index, which, turned, reverse):
        for step in range(1, blocks):

            @pl.when(has_later(step, not reverse))
            def _():
                carry_copy(index, step, reverse).wait_recv()

        slots = arrivals.shape[1]
        entering = arrivals[index].reshape(slots, state)
        level = 0
        while 1 << level < blocks:
            nearer = pltpu.roll(entering, slots - (1 << level), 0)
            matrix = power(which, local_levels + level)
            entering = entering + product(split(nearer), matrix, turned)
            level += 1
        rows = jnp.broadcast_to(entering[0:1], (8, state))
        rows = product(split(rows), power(which, 0), turned)
        exponent = 7 - row8 if reverse else row8
        for level in range(local_levels):
            further = product(split(rows), power(which, level), turned)
            if level < 3:
                rows = jnp.where((exponent >> level) % 2 == 1, further, rows)
            else:
                rows = jnp.concatenate([further, rows] if reverse else [rows, further])
        return rows

    def drain_carry(index, reverse):
        for step in range(1, blocks):

            @pl.when(has_later(step, reverse))
            def _():
                carry_copy(index, step, reverse).wait_send()

    ending = jnp.logical_and(last_block, row == frame_length - 1)

    filtered = local_scan(drive, 0, True, False)
    start_carry(0, filtered, False)
    filtered = filtered + finish_carry(0, 0, True, False)
    blended = jnp.where(ending, filtered, product(split(filtered), blend, True))
    smoothed = local_scan(blended, 1, True, True)
    start_carry(1, smoothed, True)
    smoothed = smoothed + finish_carry(1, 1, True, True)
    smoothed_out[0] = smoothed

    smoothed_pair = split(smoothed)
    miss = product(smoothed_pair, readout, True) - frames_ref[0].astype(WIDE)
    scale = 1.0 / (windows * frames_total)
    miss_pair = split(miss * scale)
    adj_smooth = local_scan(product(miss_pair, readout), 1, False, False)
    start_carry(2, adj_smooth, False)

    reduce_a = Reduction(refs_a[0].shape[0], sizes, refs_a)
    reduce_b = Reduction(refs_b[0].shape[0], sizes, refs_b)
    grad_read = inner(miss_pair, smoothed_pair)
    read_rows = 2 * state
    if refs_a[0].shape[0] > read_rows:
        refs_a[0][read_rows:] = jnp.zeros((refs_a[0].shape[0] - read_rows, 128), WIDE)
    refs_a[0][0:state] = grad_read[:, 0:128]
    refs_a[0][state:read_rows] = grad_read[:, 128:256]
    reduce_a.start_scatter(0)
    loss = jnp.sum(miss * miss, axis=0, keepdims=True)
    loss = (loss[:, 0:128] + loss[:, 128:256]) * (0.5 * scale / state)

    loss_pending = []

    def start_loss(level, value):
        loss_send[level] = value
        here = lax.axis_index(AXES[level])
        for step in range(1, sizes[level]):
            to = lax.rem(here + step, sizes[level])
            copy = remote(
                loss_send.at[level],
                loss_slots.at[level, here],
                loss_send_sem.at[level, step - 1],
                loss_recv_sem.at[level, step - 1],
                {AXES[level]: to},
            )
            copy.start()
            loss_pending.append(copy)
        loss_slots[level, here] = value

    def finish_loss(level):
        here, size = lax.axis_index(AXES[level]), sizes[level]
        for step in range(1, size):
            source = lax.rem(here + size - step, size)
            remote(
                loss_send.at[level],
                loss_slots.at[level, source],
                loss_send_sem.at[level, step - 1],
                loss_recv_sem.at[level, step - 1],
                {AXES[level]: source},
            ).wait_recv()
        value = loss_slots[level, 0]
        for index in range(1, size):
            value = value + loss_slots[level, index]
        return value

    start_loss(0, loss)
    adj_smooth = adj_smooth + finish_carry(2, 1, False, False)
    d_filtered = jnp.where(ending, adj_smooth, product(split(adj_smooth), blend))
    adj_filter = local_scan(d_filtered, 0, False, True)
    start_carry(3, adj_filter, True)
    reduce_a.finish_scatter(0)
    reduce_a.start_scatter(1)
    start_loss(1, finish_loss(0))
    adj_filter = adj_filter + finish_carry(3, 0, False, True)

    d_observed = product(split(adj_filter), gain).astype(SHORT)
    reduce_a.finish_scatter(1)
    reduce_a.start_scatter(2)
    start_loss(2, finish_loss(1))
    back = [dot(d_observed, second_ref[tap], ((1,), (1,))) for tap in range(KERNEL_TAPS)]
    pieces = [jnp.zeros((SECOND_SPACING, channels), WIDE)] * (reach // SECOND_SPACING)
    for tap in range(KERNEL_TAPS):
        for part in range(frame_length // SECOND_SPACING):
            rows = back[tap][part * SECOND_SPACING : (part + 1) * SECOND_SPACING]
            pieces[tap + part] = pieces[tap + part] + rows
    d_preact = jnp.concatenate(pieces) * slope[...]
    padded = []
    for tap in range(KERNEL_TAPS):
        before = low + (tap - 1) * FIRST_SPACING
        after = ext.shape[0] - reach - before
        padded.append(
            jnp.concatenate(
                [
                    jnp.zeros((before, channels), WIDE),
                    d_preact,
                    jnp.zeros((after, channels), WIDE),
                ]
            )
        )
    wide = split(jnp.concatenate(padded, axis=1))
    signal = ext[...]
    grad_first = dot(signal, wide[0], ((0,), (0,))) + dot(signal, wide[1], ((0,), (0,)))
    grad_second = dot(spaced, d_observed, ((0,), (0,)))
    second_rows = KERNEL_TAPS * channels
    refs_b[0][0:second_rows] = grad_second
    for tap in range(KERNEL_TAPS):
        start = second_rows + tap * state
        refs_b[0][start : start + state] = grad_first[:, tap * channels : (tap + 1) * channels]
    used = second_rows + KERNEL_TAPS * state
    if refs_b[0].shape[0] > used:
        refs_b[0][used:] = jnp.zeros((refs_b[0].shape[0] - used, 128), WIDE)

    reduce_b.start_scatter(0)
    reduce_a.finish_scatter(2)
    reduce_a.start_gather(2)
    reduce_b.finish_scatter(0)
    reduce_b.start_scatter(1)
    reduce_a.finish_gather(2)
    reduce_a.start_gather(1)
    reduce_b.finish_scatter(1)
    reduce_b.start_scatter(2)
    reduce_a.finish_gather(1)
    reduce_a.start_gather(0)
    reduce_b.finish_scatter(2)
    reduce_b.start_gather(2)
    reduce_a.finish_gather(0)
    read_out[:, 0:128] = refs_a[1][0:state].astype(WIDE)
    read_out[:, 128:256] = refs_a[1][state:read_rows].astype(WIDE)
    loss_out[0] = jnp.sum(finish_loss(2))
    reduce_b.finish_gather(2)
    reduce_b.start_gather(1)
    reduce_b.finish_gather(1)
    reduce_b.start_gather(0)
    reduce_b.finish_gather(0)
    for tap in range(KERNEL_TAPS):
        second_out[tap] = refs_b[1][tap * channels : (tap + 1) * channels].astype(WIDE)
        start = second_rows + tap * state
        first_out[tap] = refs_b[1][start : start + state].astype(WIDE)

    @pl.when(jnp.logical_not(last_block))
    def _():
        to_next().wait_send()

    @pl.when(jnp.logical_not(first_block))
    def _():
        to_previous().wait_send()

    for index in range(4):
        drain_carry(index, index % 2 == 1)
    reduce_a.drain()
    reduce_b.drain()
    for copy in loss_pending:
        copy.wait_send()


def reduction_scratch(rows, sizes, kept):
    piece, left = [], rows
    for size in sizes:
        left //= size
        piece.append(left)
    before = [rows] + piece[:-1]
    most = max(sizes)
    return [
        pltpu.VMEM((rows, 128), WIDE),
        pltpu.VMEM((rows, 128), kept),
        *[pltpu.VMEM((count, 128), SHORT) for count in before],
        *[pltpu.VMEM((size - 1, count, 128), SHORT) for size, count in zip(sizes, piece)],
        *[pltpu.VMEM((count, 128), WIDE) for count in piece[:-1]],
        pltpu.SemaphoreType.DMA((6, most)),
        pltpu.SemaphoreType.DMA((6, most)),
    ]


def body(frames, *parameters):
    cores = lax.axis_size("state")
    blocks = lax.axis_size("tm") * cores
    sizes = tuple(lax.axis_size(axis) for axis in AXES)
    frame_length, state = frames.shape[1], frames.shape[2]
    channels = parameters[1].shape[2]
    levels = frame_length.bit_length() - 1 + (blocks - 1).bit_length()
    slots = max(8, 1 << (blocks - 1).bit_length())
    unit = 16 * math.prod(sizes)
    rows_a = -(-2 * state // unit) * unit
    rows_b = -(-(KERNEL_TAPS * (state + channels)) // unit) * unit
    most = max(sizes)
    dims = (blocks, cores, sizes, frames.shape[0] * sizes[1], frame_length * blocks, levels)
    vmem = pl.BlockSpec(memory_space=pltpu.VMEM)
    return tuple(
        pl.pallas_call(
            functools.partial(kernel, dims),
            out_shape=(
                jax.ShapeDtypeStruct((1, frame_length, state), WIDE),
                jax.ShapeDtypeStruct((KERNEL_TAPS, state, channels), WIDE),
                jax.ShapeDtypeStruct((KERNEL_TAPS, channels, channels), WIDE),
                jax.ShapeDtypeStruct((state, state), WIDE),
                jax.ShapeDtypeStruct((1,), WIDE),
            ),
            in_specs=[vmem] * 8,
            out_specs=(vmem, vmem, vmem, vmem, pl.BlockSpec(memory_space=pltpu.SMEM)),
            scratch_shapes=[
                pltpu.VMEM((frame_length + 2 * EDGE, state), SHORT),
                pltpu.VMEM((2, levels, state, state), SHORT),
                pltpu.VMEM((2, levels, state, state), SHORT),
                pltpu.VMEM((4, 1, state), WIDE),
                pltpu.VMEM((4, slots, 1, state), WIDE),
                pltpu.VMEM((frame_length + 2 * SECOND_SPACING, channels), WIDE),
                pltpu.SemaphoreType.DMA((2,)),
                pltpu.SemaphoreType.DMA((2,)),
                pltpu.SemaphoreType.DMA((4, blocks)),
                pltpu.SemaphoreType.DMA((4, blocks)),
                pltpu.VMEM((3, 1, 128), WIDE),
                pltpu.VMEM((3, most, 1, 128), WIDE),
                pltpu.SemaphoreType.DMA((3, most)),
                pltpu.SemaphoreType.DMA((3, most)),
                *reduction_scratch(rows_a, sizes, SHORT),
                *reduction_scratch(rows_b, sizes, WIDE),
            ],
            compiler_params=pltpu.CompilerParams(
                collective_id=0, has_side_effects=True, vmem_limit_bytes=48 * 1024 * 1024
            ),
        )(frames, *parameters)
    )


def solution(mesh):
    return jax.shard_map(
        body,
        mesh=mesh,
        in_specs=(P(("groups", "dp"), ("tm", "state"), None), P(), P(), P(), P(), P(), P(), P()),
        out_specs=(
            P(("groups", "dp"), ("tm", "state"), None),
            P("groups", None, None),
            P("groups", None, None),
            P("groups", None),
            P("groups"),
        ),
        check_vma=False,
    )
```

```python
import functools
import math

import jax
import jax.numpy as jnp
from jax import lax
from jax.experimental import pallas as pl
from jax.experimental.pallas import tpu as pltpu
from jax.sharding import PartitionSpec as P

KERNEL_TAPS = 3
FIRST_SPACING = 8
SECOND_SPACING = 64
EDGE = 80
AXES = ("state", "dp", "tm")
SHORT, WIDE = (jnp.bfloat16, jnp.float32)


def split(array):
    high = array.astype(SHORT)
    return high, (array - high.astype(WIDE)).astype(SHORT)


def dot(a, b, contract):
    return lax.dot_general(a, b, (contract, ((), ())), preferred_element_type=WIDE)


def product(a, b, turned=False):
    contract = ((1,), (1 if turned else 0,))
    return dot(a[0], b[0], contract) + (dot(a[0], b[1], contract) + dot(a[1], b[0], contract))


def square(matrix):
    high = matrix.astype(SHORT)
    left = matrix - high.astype(WIDE)
    middle = left.astype(SHORT)
    low = (left - middle.astype(WIDE)).astype(SHORT)
    contract = ((1,), (0,))
    small = dot(high, low, contract) + dot(low, high, contract) + dot(middle, middle, contract)
    cross = dot(high, middle, contract) + dot(middle, high, contract)
    return dot(high, high, contract) + (cross + small)


def inner(a, b):
    contract = ((0,), (0,))
    return dot(a[0], b[0], contract) + (dot(a[0], b[1], contract) + dot(a[1], b[0], contract))


def remote(src, dst, send_sem, recv_sem, device):
    return pltpu.make_async_remote_copy(
        src_ref=src,
        dst_ref=dst,
        send_sem=send_sem,
        recv_sem=recv_sem,
        device_id=device,
        device_id_type=pl.DeviceIdType.MESH,
    )


class Reduction:
    def __init__(self, rows, sizes, refs):
        (self.total, self.full), self.sends, self.slots = refs[:2], refs[2:5], refs[5:8]
        self.held, (self.send_sem, self.recv_sem) = refs[8:10], refs[10:12]
        self.held = (self.total,) + tuple(self.held)
        self.sizes, self.pending = sizes, []
        self.at = [lax.axis_index(axis) for axis in AXES]
        self.piece = []
        for size in sizes:
            rows //= size
            self.piece.append(rows)

    def region(self, level, index):
        offset = index * self.piece[level]
        for above in range(level):
            offset = offset + self.at[above] * self.piece[above]
        return pl.ds(pl.multiple_of(offset, 16), self.piece[level])

    def start_scatter(self, level):
        self.sends[level][...] = self.held[level][...].astype(SHORT)
        for step in range(1, self.sizes[level]):
            to = lax.rem(self.at[level] + step, self.sizes[level])
            start = pl.multiple_of(to * self.piece[level], 16)
            copy = remote(
                self.sends[level].at[pl.ds(start, self.piece[level])],
                self.slots[level].at[step - 1],
                self.send_sem.at[level, step - 1],
                self.recv_sem.at[level, step - 1],
                {AXES[level]: to},
            )
            copy.start()
            self.pending.append(copy)

    def finish_scatter(self, level):
        for copy in self.pending[-(self.sizes[level] - 1) :]:
            copy.wait_recv()
        start = pl.multiple_of(self.at[level] * self.piece[level], 16)
        value = self.held[level][pl.ds(start, self.piece[level])]
        for step in range(1, self.sizes[level]):
            value = value + self.slots[level][step - 1].astype(WIDE)
        if level + 1 < len(AXES):
            self.held[level + 1][...] = value
        else:
            self.full[self.region(level, self.at[level])] = value.astype(self.full.dtype)

    def start_gather(self, level):
        mine = self.full.at[self.region(level, self.at[level])]
        for step in range(1, self.sizes[level]):
            to = lax.rem(self.at[level] + step, self.sizes[level])
            copy = remote(
                mine,
                mine,
                self.send_sem.at[3 + level, step - 1],
                self.recv_sem.at[3 + level, step - 1],
                {AXES[level]: to},
            )
            copy.start()
            self.pending.append(copy)

    def finish_gather(self, level):
        for step in range(1, self.sizes[level]):
            size = self.sizes[level]
            source = lax.rem(self.at[level] + size - step, size)
            theirs = self.full.at[self.region(level, source)]
            remote(
                theirs,
                theirs,
                self.send_sem.at[3 + level, step - 1],
                self.recv_sem.at[3 + level, step - 1],
                {AXES[level]: source},
            ).wait_recv()

    def drain(self):
        for copy in self.pending:
            copy.wait_send()


def kernel(dims, *refs):
    blocks, cores, sizes, windows, frames_total, levels = dims
    frames_ref, sources = refs[0], refs[1:8]
    (first_ref, second_ref, readout_ref, gain_ref) = refs[51:55]
    (transition_ref, smoother_ref, blend_ref, fetch_sem) = refs[55:59]
    (smoothed_out, first_out, second_out, read_out, loss_out) = refs[8:13]
    (ext, power_high, power_low, ends, arrivals, slope) = refs[13:19]
    (halo_send, halo_recv, carry_send, carry_recv) = refs[19:23]
    (loss_send, loss_slots, loss_send_sem, loss_recv_sem) = refs[23:27]
    refs_a, refs_b = refs[27:39], refs[39:51]
    frame_length = frames_ref.shape[1]
    state = transition_ref.shape[0]
    local_levels = frame_length.bit_length() - 1
    place = lax.axis_index("tm") * cores + lax.axis_index("state")
    first_block, last_block = place == 0, place == blocks - 1

    def device(at):
        return {"tm": at // cores, "state": lax.rem(at, cores)}

    center = ext.at[EDGE : EDGE + frame_length]
    fetches = [
        pltpu.make_async_copy(src, dst, fetch_sem.at[index])
        for index, (src, dst) in enumerate(
            zip((*sources, frames_ref.at[0]), (*refs[51:58], center))
        )
    ]
    fetch_first, fetch_second, fetch_readout, fetch_gain = fetches[:4]
    fetch_transition, fetch_smoother, fetch_blend, fetch_frames = fetches[4:]
    for fetch in (
        fetch_transition,
        fetch_frames,
        fetch_first,
        fetch_second,
        fetch_gain,
        fetch_smoother,
        fetch_blend,
        fetch_readout,
    ):
        fetch.start()
    ext[0:EDGE] = jnp.zeros((EDGE, state), SHORT)
    ext[EDGE + frame_length :] = jnp.zeros((EDGE, state), SHORT)
    arrivals[...] = jnp.zeros_like(arrivals)
    barrier = pltpu.get_barrier_semaphore()
    for step in range(1, blocks):
        pl.semaphore_signal(
            barrier,
            inc=1,
            device_id=device(lax.rem(place + step, blocks)),
            device_id_type=pl.DeviceIdType.MESH,
        )
    for step in range(1, sizes[1]):
        pl.semaphore_signal(
            barrier,
            inc=1,
            device_id={"dp": lax.rem(lax.axis_index("dp") + step, sizes[1])},
            device_id_type=pl.DeviceIdType.MESH,
        )
    pl.semaphore_wait(barrier, blocks - 1 + sizes[1] - 1)

    def to_next():
        return remote(
            frames_ref.at[0, frame_length - EDGE : frame_length],
            ext.at[0:EDGE],
            halo_send.at[0],
            halo_recv.at[0],
            device(lax.rem(place + 1, blocks)),
        )

    def to_previous():
        return remote(
            frames_ref.at[0, 0:EDGE],
            ext.at[EDGE + frame_length : 2 * EDGE + frame_length],
            halo_send.at[1],
            halo_recv.at[1],
            device(lax.rem(place + blocks - 1, blocks)),
        )

    @pl.when(jnp.logical_not(last_block))
    def _():
        to_next().start()

    @pl.when(jnp.logical_not(first_block))
    def _():
        to_previous().start()

    def power(which, level):
        return power_high[which, level], power_low[which, level]

    def store_powers(which, held, start, stop):
        for level in range(start, stop):
            power_high[which, level], power_low[which, level] = split(held)
            if level + 1 < levels:
                held = square(held)
        return held

    fetch_transition.wait()
    next_power = store_powers(0, transition_ref[...], 0, local_levels)
    fetch_first.wait()
    fetch_second.wait()
    fetch_gain.wait()
    fetch_frames.wait()
    gain = split(gain_ref[...])

    @pl.when(jnp.logical_not(first_block))
    def _():
        to_next().wait_recv()

    @pl.when(jnp.logical_not(last_block))
    def _():
        to_previous().wait_recv()

    reach = frame_length + 2 * SECOND_SPACING
    low = EDGE - SECOND_SPACING
    taps = jnp.concatenate([first_ref[tap] for tap in range(KERNEL_TAPS)], axis=1)
    partial = dot(ext[...], taps, ((1,), (0,)))
    channels = second_ref.shape[2]
    preact = sum(
        partial[
            low + (tap - 1) * FIRST_SPACING : low + (tap - 1) * FIRST_SPACING + reach,
            tap * channels : (tap + 1) * channels,
        ]
        for tap in range(KERNEL_TAPS)
    )
    where_row = lax.broadcasted_iota(jnp.int32, (reach, channels), 0)
    begin = jnp.where(first_block, SECOND_SPACING, 0)
    end = jnp.where(last_block, SECOND_SPACING + frame_length, reach)
    inside = jnp.logical_and(where_row >= begin, where_row < end)
    root = math.sqrt(2.0 / math.pi)
    squared = preact * preact
    bent = jnp.tanh(root * (preact + 0.044715 * (squared * preact)))
    half = 0.5 * (1.0 + bent)
    hidden = jnp.where(inside, preact * half, 0.0).astype(SHORT)
    bend = 0.5 * preact * (1.0 - bent * bent) * (root * (1.0 + 3 * 0.044715 * squared))
    slope[...] = jnp.where(inside, half + bend, 0.0)
    spaced = jnp.concatenate(
        [
            hidden[tap * SECOND_SPACING : tap * SECOND_SPACING + frame_length]
            for tap in range(KERNEL_TAPS)
        ],
        axis=1,
    )
    second = jnp.concatenate([second_ref[tap] for tap in range(KERNEL_TAPS)], axis=0)
    observed = dot(spaced, second, ((1,), (0,)))
    drive = product(split(observed), gain, True)

    row = lax.broadcasted_iota(jnp.int32, (frame_length, state), 0)
    row8 = lax.broadcasted_iota(jnp.int32, (8, state), 0)

    def local_scan(running, which, turned, reverse):
        for level in range(local_levels):
            stride = 1 << level
            matrix = power(which, level)
            if stride < 8:
                moved = pltpu.roll(running, frame_length - stride if reverse else stride, 0)
                kept = row < frame_length - stride if reverse else row >= stride
                moved = jnp.where(kept, moved, 0.0)
                running = running + product(split(moved), matrix, turned)
            elif reverse:
                added = product(split(running[stride:]), matrix, turned)
                running = jnp.concatenate(
                    [running[: frame_length - stride] + added, running[frame_length - stride :]]
                )
            else:
                added = product(split(running[: frame_length - stride]), matrix, turned)
                running = jnp.concatenate([running[:stride], running[stride:] + added])
        return running

    def carry_copy(index, step, reverse):
        to = lax.rem(place + (blocks - step if reverse else step), blocks)
        return remote(
            ends.at[index],
            arrivals.at[index, step - 1],
            carry_send.at[index, step - 1],
            carry_recv.at[index, step - 1],
            device(to),
        )

    def has_later(step, reverse):
        return place >= step if reverse else place + step < blocks

    def start_carry(index, running, reverse):
        ends[index] = running[0:1] if reverse else running[frame_length - 1 :]
        for step in range(1, blocks):

            @pl.when(has_later(step, reverse))
            def _():
                carry_copy(index, step, reverse).start()

    def finish_carry(index, which, turned, reverse):
        for step in range(1, blocks):

            @pl.when(has_later(step, not reverse))
            def _():
                carry_copy(index, step, reverse).wait_recv()

        slots = arrivals.shape[1]
        entering = arrivals[index].reshape(slots, state)
        level = 0
        while 1 << level < blocks:
            nearer = pltpu.roll(entering, slots - (1 << level), 0)
            matrix = power(which, local_levels + level)
            entering = entering + product(split(nearer), matrix, turned)
            level += 1
        rows = jnp.broadcast_to(entering[0:1], (8, state))
        rows = product(split(rows), power(which, 0), turned)
        exponent = 7 - row8 if reverse else row8
        for level in range(local_levels):
            further = product(split(rows), power(which, level), turned)
            if level < 3:
                rows = jnp.where((exponent >> level) % 2 == 1, further, rows)
            else:
                rows = jnp.concatenate([further, rows] if reverse else [rows, further])
        return rows

    def drain_carry(index, reverse):
        for step in range(1, blocks):

            @pl.when(has_later(step, reverse))
            def _():
                carry_copy(index, step, reverse).wait_send()

    ending = jnp.logical_and(last_block, row == frame_length - 1)

    filtered = local_scan(drive, 0, True, False)
    start_carry(0, filtered, False)
    store_powers(0, next_power, local_levels, levels)
    fetch_smoother.wait()
    store_powers(1, smoother_ref[...], 0, levels)
    fetch_blend.wait()
    fetch_readout.wait()
    blend, readout = split(blend_ref[...]), split(readout_ref[...])
    filtered = filtered + finish_carry(0, 0, True, False)
    blended = jnp.where(ending, filtered, product(split(filtered), blend, True))
    smoothed = local_scan(blended, 1, True, True)
    start_carry(1, smoothed, True)
    smoothed = smoothed + finish_carry(1, 1, True, True)
    smoothed_out[0] = smoothed

    smoothed_pair = split(smoothed)
    miss = product(smoothed_pair, readout, True) - center[...].astype(WIDE)
    scale = 1.0 / (windows * frames_total)
    miss_pair = split(miss * scale)
    adj_smooth = local_scan(product(miss_pair, readout), 1, False, False)
    start_carry(2, adj_smooth, False)

    reduce_a = Reduction(refs_a[0].shape[0], sizes, refs_a)
    reduce_b = Reduction(refs_b[0].shape[0], sizes, refs_b)
    grad_read = inner(miss_pair, smoothed_pair)
    read_rows = 2 * state
    if refs_a[0].shape[0] > read_rows:
        refs_a[0][read_rows:] = jnp.zeros((refs_a[0].shape[0] - read_rows, 128), WIDE)
    refs_a[0][0:state] = grad_read[:, 0:128]
    refs_a[0][state:read_rows] = grad_read[:, 128:256]
    reduce_a.start_scatter(0)
    loss = jnp.sum(miss * miss, axis=0, keepdims=True)
    loss = (loss[:, 0:128] + loss[:, 128:256]) * (0.5 * scale / state)

    loss_pending = []

    def start_loss(level, value):
        loss_send[level] = value
        here = lax.axis_index(AXES[level])
        for step in range(1, sizes[level]):
            to = lax.rem(here + step, sizes[level])
            copy = remote(
                loss_send.at[level],
                loss_slots.at[level, here],
                loss_send_sem.at[level, step - 1],
                loss_recv_sem.at[level, step - 1],
                {AXES[level]: to},
            )
            copy.start()
            loss_pending.append(copy)
        loss_slots[level, here] = value

    def finish_loss(level):
        here, size = lax.axis_index(AXES[level]), sizes[level]
        for step in range(1, size):
            source = lax.rem(here + size - step, size)
            remote(
                loss_send.at[level],
                loss_slots.at[level, source],
                loss_send_sem.at[level, step - 1],
                loss_recv_sem.at[level, step - 1],
                {AXES[level]: source},
            ).wait_recv()
        value = loss_slots[level, 0]
        for index in range(1, size):
            value = value + loss_slots[level, index]
        return value

    start_loss(0, loss)
    adj_smooth = adj_smooth + finish_carry(2, 1, False, False)
    d_filtered = jnp.where(ending, adj_smooth, product(split(adj_smooth), blend))
    adj_filter = local_scan(d_filtered, 0, False, True)
    start_carry(3, adj_filter, True)
    reduce_a.finish_scatter(0)
    reduce_a.start_scatter(1)
    start_loss(1, finish_loss(0))
    adj_filter = adj_filter + finish_carry(3, 0, False, True)

    d_observed = product(split(adj_filter), gain).astype(SHORT)
    reduce_a.finish_scatter(1)
    reduce_a.start_scatter(2)
    start_loss(2, finish_loss(1))
    back = [dot(d_observed, second_ref[tap], ((1,), (1,))) for tap in range(KERNEL_TAPS)]
    pieces = [jnp.zeros((SECOND_SPACING, channels), WIDE)] * (reach // SECOND_SPACING)
    for tap in range(KERNEL_TAPS):
        for part in range(frame_length // SECOND_SPACING):
            rows = back[tap][part * SECOND_SPACING : (part + 1) * SECOND_SPACING]
            pieces[tap + part] = pieces[tap + part] + rows
    d_preact = jnp.concatenate(pieces) * slope[...]
    padded = []
    for tap in range(KERNEL_TAPS):
        before = low + (tap - 1) * FIRST_SPACING
        after = ext.shape[0] - reach - before
        padded.append(
            jnp.concatenate(
                [
                    jnp.zeros((before, channels), WIDE),
                    d_preact,
                    jnp.zeros((after, channels), WIDE),
                ]
            )
        )
    wide = split(jnp.concatenate(padded, axis=1))
    signal = ext[...]
    grad_first = dot(signal, wide[0], ((0,), (0,))) + dot(signal, wide[1], ((0,), (0,)))
    grad_second = dot(spaced, d_observed, ((0,), (0,)))
    second_rows = KERNEL_TAPS * channels
    refs_b[0][0:second_rows] = grad_second
    for tap in range(KERNEL_TAPS):
        start = second_rows + tap * state
        refs_b[0][start : start + state] = grad_first[:, tap * channels : (tap + 1) * channels]
    used = second_rows + KERNEL_TAPS * state
    if refs_b[0].shape[0] > used:
        refs_b[0][used:] = jnp.zeros((refs_b[0].shape[0] - used, 128), WIDE)

    reduce_b.start_scatter(0)
    reduce_a.finish_scatter(2)
    reduce_a.start_gather(2)
    reduce_b.finish_scatter(0)
    reduce_b.start_scatter(1)
    reduce_a.finish_gather(2)
    reduce_a.start_gather(1)
    reduce_b.finish_scatter(1)
    reduce_b.start_scatter(2)
    reduce_a.finish_gather(1)
    reduce_a.start_gather(0)
    reduce_b.finish_scatter(2)
    reduce_b.start_gather(2)
    reduce_a.finish_gather(0)
    read_out[:, 0:128] = refs_a[1][0:state].astype(WIDE)
    read_out[:, 128:256] = refs_a[1][state:read_rows].astype(WIDE)
    loss_out[0] = jnp.sum(finish_loss(2))
    reduce_b.finish_gather(2)
    reduce_b.start_gather(1)
    reduce_b.finish_gather(1)
    reduce_b.start_gather(0)
    reduce_b.finish_gather(0)
    for tap in range(KERNEL_TAPS):
        second_out[tap] = refs_b[1][tap * channels : (tap + 1) * channels].astype(WIDE)
        start = second_rows + tap * state
        first_out[tap] = refs_b[1][start : start + state].astype(WIDE)

    @pl.when(jnp.logical_not(last_block))
    def _():
        to_next().wait_send()

    @pl.when(jnp.logical_not(first_block))
    def _():
        to_previous().wait_send()

    for index in range(4):
        drain_carry(index, index % 2 == 1)
    reduce_a.drain()
    reduce_b.drain()
    for copy in loss_pending:
        copy.wait_send()


def reduction_scratch(rows, sizes, kept):
    piece, left = [], rows
    for size in sizes:
        left //= size
        piece.append(left)
    before = [rows] + piece[:-1]
    most = max(sizes)
    return [
        pltpu.VMEM((rows, 128), WIDE),
        pltpu.VMEM((rows, 128), kept),
        *[pltpu.VMEM((count, 128), SHORT) for count in before],
        *[pltpu.VMEM((size - 1, count, 128), SHORT) for size, count in zip(sizes, piece)],
        *[pltpu.VMEM((count, 128), WIDE) for count in piece[:-1]],
        pltpu.SemaphoreType.DMA((6, most)),
        pltpu.SemaphoreType.DMA((6, most)),
    ]


def body(frames, *parameters):
    cores = lax.axis_size("state")
    blocks = lax.axis_size("tm") * cores
    sizes = tuple(lax.axis_size(axis) for axis in AXES)
    frame_length, state = frames.shape[1], frames.shape[2]
    hbm = pl.BlockSpec(memory_space=pltpu.HBM)
    channels = parameters[1].shape[2]
    levels = frame_length.bit_length() - 1 + (blocks - 1).bit_length()
    slots = max(8, 1 << (blocks - 1).bit_length())
    unit = 16 * math.prod(sizes)
    rows_a = -(-2 * state // unit) * unit
    rows_b = -(-(KERNEL_TAPS * (state + channels)) // unit) * unit
    most = max(sizes)
    dims = (blocks, cores, sizes, frames.shape[0] * sizes[1], frame_length * blocks, levels)
    vmem = pl.BlockSpec(memory_space=pltpu.VMEM)
    return tuple(
        pl.pallas_call(
            functools.partial(kernel, dims),
            out_shape=(
                jax.ShapeDtypeStruct((1, frame_length, state), WIDE),
                jax.ShapeDtypeStruct((KERNEL_TAPS, state, channels), WIDE),
                jax.ShapeDtypeStruct((KERNEL_TAPS, channels, channels), WIDE),
                jax.ShapeDtypeStruct((state, state), WIDE),
                jax.ShapeDtypeStruct((1,), WIDE),
            ),
            in_specs=[hbm] * 8,
            out_specs=(vmem, vmem, vmem, vmem, pl.BlockSpec(memory_space=pltpu.SMEM)),
            scratch_shapes=[
                pltpu.VMEM((frame_length + 2 * EDGE, state), SHORT),
                pltpu.VMEM((2, levels, state, state), SHORT),
                pltpu.VMEM((2, levels, state, state), SHORT),
                pltpu.VMEM((4, 1, state), WIDE),
                pltpu.VMEM((4, slots, 1, state), WIDE),
                pltpu.VMEM((frame_length + 2 * SECOND_SPACING, channels), WIDE),
                pltpu.SemaphoreType.DMA((2,)),
                pltpu.SemaphoreType.DMA((2,)),
                pltpu.SemaphoreType.DMA((4, blocks)),
                pltpu.SemaphoreType.DMA((4, blocks)),
                pltpu.VMEM((3, 1, 128), WIDE),
                pltpu.VMEM((3, most, 1, 128), WIDE),
                pltpu.SemaphoreType.DMA((3, most)),
                pltpu.SemaphoreType.DMA((3, most)),
                *reduction_scratch(rows_a, sizes, SHORT),
                *reduction_scratch(rows_b, sizes, WIDE),
                *[pltpu.VMEM(array.shape, array.dtype) for array in parameters],
                pltpu.SemaphoreType.DMA((8,)),
            ],
            compiler_params=pltpu.CompilerParams(
                collective_id=0, has_side_effects=True, vmem_limit_bytes=48 * 1024 * 1024
            ),
        )(frames, *parameters)
    )


def solution(mesh):
    return jax.shard_map(
        body,
        mesh=mesh,
        in_specs=(P(("groups", "dp"), ("tm", "state"), None), P(), P(), P(), P(), P(), P(), P()),
        out_specs=(
            P(("groups", "dp"), ("tm", "state"), None),
            P("groups", None, None),
            P("groups", None, None),
            P("groups", None),
            P("groups"),
        ),
        check_vma=False,
    )
```

```python
import functools
import math

import jax
import jax.numpy as jnp
from jax import lax
from jax.experimental import pallas as pl
from jax.experimental.pallas import tpu as pltpu
from jax.sharding import PartitionSpec as P

KERNEL_TAPS = 3
FIRST_SPACING = 8
SECOND_SPACING = 64
EDGE = 80
AXES = ("state", "dp", "tm")
SHORT, WIDE = (jnp.bfloat16, jnp.float32)


def split(array):
    high = array.astype(SHORT)
    return high, (array - high.astype(WIDE)).astype(SHORT)


def dot(a, b, contract):
    return lax.dot_general(a, b, (contract, ((), ())), preferred_element_type=WIDE)


def product(a, b, turned=False):
    contract = ((1,), (1 if turned else 0,))
    return dot(a[0], b[0], contract) + (dot(a[0], b[1], contract) + dot(a[1], b[0], contract))


def square(matrix):
    high = matrix.astype(SHORT)
    left = matrix - high.astype(WIDE)
    middle = left.astype(SHORT)
    low = (left - middle.astype(WIDE)).astype(SHORT)
    contract = ((1,), (0,))
    small = dot(high, low, contract) + dot(low, high, contract) + dot(middle, middle, contract)
    cross = dot(high, middle, contract) + dot(middle, high, contract)
    return dot(high, high, contract) + (cross + small)


def inner(a, b):
    contract = ((0,), (0,))
    return dot(a[0], b[0], contract) + (dot(a[0], b[1], contract) + dot(a[1], b[0], contract))


def remote(src, dst, send_sem, recv_sem, device):
    return pltpu.make_async_remote_copy(
        src_ref=src,
        dst_ref=dst,
        send_sem=send_sem,
        recv_sem=recv_sem,
        device_id=device,
        device_id_type=pl.DeviceIdType.MESH,
    )


class Reduction:
    def __init__(self, rows, sizes, refs):
        (self.total, self.full), self.sends, self.slots = refs[:2], refs[2:5], refs[5:8]
        self.held, (self.send_sem, self.recv_sem) = refs[8:10], refs[10:12]
        self.held = (self.total,) + tuple(self.held)
        self.sizes, self.pending = sizes, []
        self.at = [lax.axis_index(axis) for axis in AXES]
        self.piece = []
        for size in sizes:
            rows //= size
            self.piece.append(rows)

    def region(self, level, index):
        offset = index * self.piece[level]
        for above in range(level):
            offset = offset + self.at[above] * self.piece[above]
        return pl.ds(pl.multiple_of(offset, 16), self.piece[level])

    def start_scatter(self, level):
        self.sends[level][...] = self.held[level][...].astype(SHORT)
        for step in range(1, self.sizes[level]):
            to = lax.rem(self.at[level] + step, self.sizes[level])
            start = pl.multiple_of(to * self.piece[level], 16)
            copy = remote(
                self.sends[level].at[pl.ds(start, self.piece[level])],
                self.slots[level].at[step - 1],
                self.send_sem.at[level, step - 1],
                self.recv_sem.at[level, step - 1],
                {AXES[level]: to},
            )
            copy.start()
            self.pending.append(copy)

    def finish_scatter(self, level):
        for copy in self.pending[-(self.sizes[level] - 1) :]:
            copy.wait_recv()
        start = pl.multiple_of(self.at[level] * self.piece[level], 16)
        value = self.held[level][pl.ds(start, self.piece[level])]
        for step in range(1, self.sizes[level]):
            value = value + self.slots[level][step - 1].astype(WIDE)
        if level + 1 < len(AXES):
            self.held[level + 1][...] = value
        else:
            self.full[self.region(level, self.at[level])] = value.astype(self.full.dtype)

    def start_gather(self, level):
        mine = self.full.at[self.region(level, self.at[level])]
        for step in range(1, self.sizes[level]):
            to = lax.rem(self.at[level] + step, self.sizes[level])
            copy = remote(
                mine,
                mine,
                self.send_sem.at[3 + level, step - 1],
                self.recv_sem.at[3 + level, step - 1],
                {AXES[level]: to},
            )
            copy.start()
            self.pending.append(copy)

    def finish_gather(self, level):
        for step in range(1, self.sizes[level]):
            size = self.sizes[level]
            source = lax.rem(self.at[level] + size - step, size)
            theirs = self.full.at[self.region(level, source)]
            remote(
                theirs,
                theirs,
                self.send_sem.at[3 + level, step - 1],
                self.recv_sem.at[3 + level, step - 1],
                {AXES[level]: source},
            ).wait_recv()

    def drain(self):
        for copy in self.pending:
            copy.wait_send()


def kernel(dims, *refs):
    blocks, cores, sizes, windows, frames_total, levels = dims
    frames_ref, sources = refs[0], refs[1:8]
    (first_ref, second_ref, readout_ref, gain_ref) = refs[51:55]
    (transition_ref, smoother_ref, blend_ref, fetch_sem) = refs[55:59]
    (smoothed_out, first_out, second_out, read_out, loss_out) = refs[8:13]
    (ext, power_high, power_low, ends, arrivals, slope) = refs[13:19]
    (halo_send, halo_recv, carry_send, carry_recv) = refs[19:23]
    (loss_send, loss_slots, loss_send_sem, loss_recv_sem) = refs[23:27]
    refs_a, refs_b = refs[27:39], refs[39:51]
    frame_length = frames_ref.shape[1]
    state = transition_ref.shape[0]
    local_levels = frame_length.bit_length() - 1
    place = lax.axis_index("tm") * cores + lax.axis_index("state")
    first_block, last_block = place == 0, place == blocks - 1

    def device(at):
        return {"tm": at // cores, "state": lax.rem(at, cores)}

    center = ext.at[EDGE : EDGE + frame_length]
    fetches = [
        pltpu.make_async_copy(src, dst, fetch_sem.at[index])
        for index, (src, dst) in enumerate(
            zip((*sources, frames_ref.at[0]), (*refs[51:58], center))
        )
    ]
    fetch_first, fetch_second, fetch_readout, fetch_gain = fetches[:4]
    fetch_transition, fetch_smoother, fetch_blend, fetch_frames = fetches[4:]
    for fetch in (
        fetch_transition,
        fetch_frames,
        fetch_first,
        fetch_second,
        fetch_gain,
        fetch_smoother,
        fetch_blend,
        fetch_readout,
    ):
        fetch.start()
    ext[0:EDGE] = jnp.zeros((EDGE, state), SHORT)
    ext[EDGE + frame_length :] = jnp.zeros((EDGE, state), SHORT)
    arrivals[...] = jnp.zeros_like(arrivals)
    barrier = pltpu.get_barrier_semaphore()
    for step in range(1, blocks):
        pl.semaphore_signal(
            barrier,
            inc=1,
            device_id=device(lax.rem(place + step, blocks)),
            device_id_type=pl.DeviceIdType.MESH,
        )
    for step in range(1, sizes[1]):
        pl.semaphore_signal(
            barrier,
            inc=1,
            device_id={"dp": lax.rem(lax.axis_index("dp") + step, sizes[1])},
            device_id_type=pl.DeviceIdType.MESH,
        )
    pl.semaphore_wait(barrier, blocks - 1 + sizes[1] - 1)

    def to_next():
        return remote(
            frames_ref.at[0, frame_length - EDGE : frame_length],
            ext.at[0:EDGE],
            halo_send.at[0],
            halo_recv.at[0],
            device(lax.rem(place + 1, blocks)),
        )

    def to_previous():
        return remote(
            frames_ref.at[0, 0:EDGE],
            ext.at[EDGE + frame_length : 2 * EDGE + frame_length],
            halo_send.at[1],
            halo_recv.at[1],
            device(lax.rem(place + blocks - 1, blocks)),
        )

    @pl.when(jnp.logical_not(last_block))
    def _():
        to_next().start()

    @pl.when(jnp.logical_not(first_block))
    def _():
        to_previous().start()

    def power(which, level):
        return power_high[which, level], power_low[which, level]

    def store_powers(which, held, start, stop):
        for level in range(start, stop):
            power_high[which, level], power_low[which, level] = split(held)
            if level + 1 < levels:
                held = square(held)
        return held

    fetch_transition.wait()
    next_power = store_powers(0, transition_ref[...], 0, local_levels)
    fetch_first.wait()
    fetch_second.wait()
    fetch_gain.wait()
    fetch_frames.wait()
    gain = split(gain_ref[...])

    @pl.when(jnp.logical_not(first_block))
    def _():
        to_next().wait_recv()

    @pl.when(jnp.logical_not(last_block))
    def _():
        to_previous().wait_recv()

    reach = frame_length + 2 * SECOND_SPACING
    low = EDGE - SECOND_SPACING
    taps = jnp.concatenate([first_ref[tap] for tap in range(KERNEL_TAPS)], axis=1)
    partial = dot(ext[...], taps, ((1,), (0,)))
    channels = second_ref.shape[2]
    preact = sum(
        partial[
            low + (tap - 1) * FIRST_SPACING : low + (tap - 1) * FIRST_SPACING + reach,
            tap * channels : (tap + 1) * channels,
        ]
        for tap in range(KERNEL_TAPS)
    )
    where_row = lax.broadcasted_iota(jnp.int32, (reach, channels), 0)
    begin = jnp.where(first_block, SECOND_SPACING, 0)
    end = jnp.where(last_block, SECOND_SPACING + frame_length, reach)
    inside = jnp.logical_and(where_row >= begin, where_row < end)
    root = math.sqrt(2.0 / math.pi)
    squared = preact * preact
    bent = jnp.tanh(root * (preact + 0.044715 * (squared * preact)))
    half = 0.5 * (1.0 + bent)
    hidden = jnp.where(inside, preact * half, 0.0).astype(SHORT)
    bend = 0.5 * preact * (1.0 - bent * bent) * (root * (1.0 + 3 * 0.044715 * squared))
    slope[...] = jnp.where(inside, half + bend, 0.0)
    spaced = jnp.concatenate(
        [
            hidden[tap * SECOND_SPACING : tap * SECOND_SPACING + frame_length]
            for tap in range(KERNEL_TAPS)
        ],
        axis=1,
    )
    second = jnp.concatenate([second_ref[tap] for tap in range(KERNEL_TAPS)], axis=0)
    observed = dot(spaced, second, ((1,), (0,)))
    drive = product(split(observed), gain, True)

    row = lax.broadcasted_iota(jnp.int32, (frame_length, state), 0)
    row8 = lax.broadcasted_iota(jnp.int32, (8, state), 0)

    def local_scan(running, which, turned, reverse):
        for level in range(local_levels):
            stride = 1 << level
            matrix = power(which, level)
            if stride < 8:
                moved = pltpu.roll(running, frame_length - stride if reverse else stride, 0)
                kept = row < frame_length - stride if reverse else row >= stride
                moved = jnp.where(kept, moved, 0.0)
                running = running + product(split(moved), matrix, turned)
            elif reverse:
                added = product(split(running[stride:]), matrix, turned)
                running = jnp.concatenate(
                    [running[: frame_length - stride] + added, running[frame_length - stride :]]
                )
            else:
                added = product(split(running[: frame_length - stride]), matrix, turned)
                running = jnp.concatenate([running[:stride], running[stride:] + added])
        return running

    def carry_copy(index, step, reverse):
        to = lax.rem(place + (blocks - step if reverse else step), blocks)
        return remote(
            ends.at[index],
            arrivals.at[index, step - 1],
            carry_send.at[index, step - 1],
            carry_recv.at[index, step - 1],
            device(to),
        )

    def has_later(step, reverse):
        return place >= step if reverse else place + step < blocks

    def start_carry(index, running, reverse):
        ends[index] = running[0:1] if reverse else running[frame_length - 1 :]
        for step in range(1, blocks):

            @pl.when(has_later(step, reverse))
            def _():
                carry_copy(index, step, reverse).start()

    def finish_carry(index, which, turned, reverse):
        for step in range(1, blocks):

            @pl.when(has_later(step, not reverse))
            def _():
                carry_copy(index, step, reverse).wait_recv()

        slots = arrivals.shape[1]
        entering = arrivals[index].reshape(slots, state)
        level = 0
        while 1 << level < blocks:
            nearer = pltpu.roll(entering, slots - (1 << level), 0)
            matrix = power(which, local_levels + level)
            entering = entering + product(split(nearer), matrix, turned)
            level += 1
        rows = jnp.broadcast_to(entering[0:1], (8, state))
        rows = product(split(rows), power(which, 0), turned)
        exponent = 7 - row8 if reverse else row8
        for level in range(local_levels):
            further = product(split(rows), power(which, level), turned)
            if level < 3:
                rows = jnp.where((exponent >> level) % 2 == 1, further, rows)
            else:
                rows = jnp.concatenate([further, rows] if reverse else [rows, further])
        return rows

    def drain_carry(index, reverse):
        for step in range(1, blocks):

            @pl.when(has_later(step, reverse))
            def _():
                carry_copy(index, step, reverse).wait_send()

    ending = jnp.logical_and(last_block, row == frame_length - 1)

    filtered = local_scan(drive, 0, True, False)
    start_carry(0, filtered, False)
    store_powers(0, next_power, local_levels, levels)
    fetch_smoother.wait()
    store_powers(1, smoother_ref[...], 0, levels)
    fetch_blend.wait()
    fetch_readout.wait()
    blend, readout = split(blend_ref[...]), split(readout_ref[...])
    filtered = filtered + finish_carry(0, 0, True, False)
    blended = jnp.where(ending, filtered, product(split(filtered), blend, True))
    smoothed = local_scan(blended, 1, True, True)
    start_carry(1, smoothed, True)
    smoothed = smoothed + finish_carry(1, 1, True, True)
    smoothed_out[0] = smoothed

    smoothed_pair = split(smoothed)
    miss = product(smoothed_pair, readout, True) - center[...].astype(WIDE)
    scale = 1.0 / (windows * frames_total)
    miss_pair = split(miss * scale)
    adj_smooth = local_scan(product(miss_pair, readout), 1, False, False)
    start_carry(2, adj_smooth, False)

    reduce_a = Reduction(refs_a[0].shape[0], sizes, refs_a)
    reduce_b = Reduction(refs_b[0].shape[0], sizes, refs_b)
    grad_read = inner(miss_pair, smoothed_pair)
    read_rows = 2 * state
    if refs_a[0].shape[0] > read_rows:
        refs_a[0][read_rows:] = jnp.zeros((refs_a[0].shape[0] - read_rows, 128), WIDE)
    refs_a[0][0:state] = grad_read[:, 0:128]
    refs_a[0][state:read_rows] = grad_read[:, 128:256]
    reduce_a.start_scatter(0)
    loss = jnp.sum(miss * miss, axis=0, keepdims=True)
    loss = (loss[:, 0:128] + loss[:, 128:256]) * (0.5 * scale / state)

    loss_pending = []

    def start_loss(level, value):
        loss_send[level] = value
        here = lax.axis_index(AXES[level])
        for step in range(1, sizes[level]):
            to = lax.rem(here + step, sizes[level])
            copy = remote(
                loss_send.at[level],
                loss_slots.at[level, here],
                loss_send_sem.at[level, step - 1],
                loss_recv_sem.at[level, step - 1],
                {AXES[level]: to},
            )
            copy.start()
            loss_pending.append(copy)
        loss_slots[level, here] = value

    def finish_loss(level):
        here, size = lax.axis_index(AXES[level]), sizes[level]
        for step in range(1, size):
            source = lax.rem(here + size - step, size)
            remote(
                loss_send.at[level],
                loss_slots.at[level, source],
                loss_send_sem.at[level, step - 1],
                loss_recv_sem.at[level, step - 1],
                {AXES[level]: source},
            ).wait_recv()
        value = loss_slots[level, 0]
        for index in range(1, size):
            value = value + loss_slots[level, index]
        return value

    start_loss(0, loss)
    adj_smooth = adj_smooth + finish_carry(2, 1, False, False)
    d_filtered = jnp.where(ending, adj_smooth, product(split(adj_smooth), blend))
    adj_filter = local_scan(d_filtered, 0, False, True)
    start_carry(3, adj_filter, True)
    signal = ext[...].astype(WIDE).T.astype(SHORT)
    spaced = spaced.astype(WIDE).T.astype(SHORT)
    reduce_a.finish_scatter(0)
    reduce_a.start_scatter(1)
    start_loss(1, finish_loss(0))
    adj_filter = adj_filter + finish_carry(3, 0, False, True)

    d_observed = product(split(adj_filter), gain).astype(SHORT)
    reduce_a.finish_scatter(1)
    reduce_a.start_scatter(2)
    start_loss(2, finish_loss(1))
    back = [dot(d_observed, second_ref[tap], ((1,), (1,))) for tap in range(KERNEL_TAPS)]
    pieces = [jnp.zeros((SECOND_SPACING, channels), WIDE)] * (reach // SECOND_SPACING)
    for tap in range(KERNEL_TAPS):
        for part in range(frame_length // SECOND_SPACING):
            rows = back[tap][part * SECOND_SPACING : (part + 1) * SECOND_SPACING]
            pieces[tap + part] = pieces[tap + part] + rows
    d_preact = jnp.concatenate(pieces) * slope[...]
    padded = []
    for tap in range(KERNEL_TAPS):
        before = low + (tap - 1) * FIRST_SPACING
        after = ext.shape[0] - reach - before
        padded.append(
            jnp.concatenate(
                [
                    jnp.zeros((before, channels), WIDE),
                    d_preact,
                    jnp.zeros((after, channels), WIDE),
                ]
            )
        )
    wide = split(jnp.concatenate(padded, axis=1))
    grad_first = dot(signal, wide[0], ((1,), (0,))) + dot(signal, wide[1], ((1,), (0,)))
    grad_second = dot(spaced, d_observed, ((1,), (0,)))
    second_rows = KERNEL_TAPS * channels
    refs_b[0][0:second_rows] = grad_second
    for tap in range(KERNEL_TAPS):
        start = second_rows + tap * state
        refs_b[0][start : start + state] = grad_first[:, tap * channels : (tap + 1) * channels]
    used = second_rows + KERNEL_TAPS * state
    if refs_b[0].shape[0] > used:
        refs_b[0][used:] = jnp.zeros((refs_b[0].shape[0] - used, 128), WIDE)

    reduce_b.start_scatter(0)
    reduce_a.finish_scatter(2)
    reduce_a.start_gather(2)
    reduce_b.finish_scatter(0)
    reduce_b.start_scatter(1)
    reduce_a.finish_gather(2)
    reduce_a.start_gather(1)
    reduce_b.finish_scatter(1)
    reduce_b.start_scatter(2)
    reduce_a.finish_gather(1)
    reduce_a.start_gather(0)
    reduce_b.finish_scatter(2)
    reduce_b.start_gather(2)
    reduce_a.finish_gather(0)
    read_out[:, 0:128] = refs_a[1][0:state].astype(WIDE)
    read_out[:, 128:256] = refs_a[1][state:read_rows].astype(WIDE)
    loss_out[0] = jnp.sum(finish_loss(2))
    reduce_b.finish_gather(2)
    reduce_b.start_gather(1)
    reduce_b.finish_gather(1)
    reduce_b.start_gather(0)
    reduce_b.finish_gather(0)
    for tap in range(KERNEL_TAPS):
        second_out[tap] = refs_b[1][tap * channels : (tap + 1) * channels].astype(WIDE)
        start = second_rows + tap * state
        first_out[tap] = refs_b[1][start : start + state].astype(WIDE)

    @pl.when(jnp.logical_not(last_block))
    def _():
        to_next().wait_send()

    @pl.when(jnp.logical_not(first_block))
    def _():
        to_previous().wait_send()

    for index in range(4):
        drain_carry(index, index % 2 == 1)
    reduce_a.drain()
    reduce_b.drain()
    for copy in loss_pending:
        copy.wait_send()


def reduction_scratch(rows, sizes, kept):
    piece, left = [], rows
    for size in sizes:
        left //= size
        piece.append(left)
    before = [rows] + piece[:-1]
    most = max(sizes)
    return [
        pltpu.VMEM((rows, 128), WIDE),
        pltpu.VMEM((rows, 128), kept),
        *[pltpu.VMEM((count, 128), SHORT) for count in before],
        *[pltpu.VMEM((size - 1, count, 128), SHORT) for size, count in zip(sizes, piece)],
        *[pltpu.VMEM((count, 128), WIDE) for count in piece[:-1]],
        pltpu.SemaphoreType.DMA((6, most)),
        pltpu.SemaphoreType.DMA((6, most)),
    ]


def body(frames, *parameters):
    cores = lax.axis_size("state")
    blocks = lax.axis_size("tm") * cores
    sizes = tuple(lax.axis_size(axis) for axis in AXES)
    frame_length, state = frames.shape[1], frames.shape[2]
    hbm = pl.BlockSpec(memory_space=pltpu.HBM)
    channels = parameters[1].shape[2]
    levels = frame_length.bit_length() - 1 + (blocks - 1).bit_length()
    slots = max(8, 1 << (blocks - 1).bit_length())
    unit = 16 * math.prod(sizes)
    rows_a = -(-2 * state // unit) * unit
    rows_b = -(-(KERNEL_TAPS * (state + channels)) // unit) * unit
    most = max(sizes)
    dims = (blocks, cores, sizes, frames.shape[0] * sizes[1], frame_length * blocks, levels)
    vmem = pl.BlockSpec(memory_space=pltpu.VMEM)
    return tuple(
        pl.pallas_call(
            functools.partial(kernel, dims),
            out_shape=(
                jax.ShapeDtypeStruct((1, frame_length, state), WIDE),
                jax.ShapeDtypeStruct((KERNEL_TAPS, state, channels), WIDE),
                jax.ShapeDtypeStruct((KERNEL_TAPS, channels, channels), WIDE),
                jax.ShapeDtypeStruct((state, state), WIDE),
                jax.ShapeDtypeStruct((1,), WIDE),
            ),
            in_specs=[hbm] * 8,
            out_specs=(vmem, vmem, vmem, vmem, pl.BlockSpec(memory_space=pltpu.SMEM)),
            scratch_shapes=[
                pltpu.VMEM((frame_length + 2 * EDGE, state), SHORT),
                pltpu.VMEM((2, levels, state, state), SHORT),
                pltpu.VMEM((2, levels, state, state), SHORT),
                pltpu.VMEM((4, 1, state), WIDE),
                pltpu.VMEM((4, slots, 1, state), WIDE),
                pltpu.VMEM((frame_length + 2 * SECOND_SPACING, channels), WIDE),
                pltpu.SemaphoreType.DMA((2,)),
                pltpu.SemaphoreType.DMA((2,)),
                pltpu.SemaphoreType.DMA((4, blocks)),
                pltpu.SemaphoreType.DMA((4, blocks)),
                pltpu.VMEM((3, 1, 128), WIDE),
                pltpu.VMEM((3, most, 1, 128), WIDE),
                pltpu.SemaphoreType.DMA((3, most)),
                pltpu.SemaphoreType.DMA((3, most)),
                *reduction_scratch(rows_a, sizes, SHORT),
                *reduction_scratch(rows_b, sizes, WIDE),
                *[pltpu.VMEM(array.shape, array.dtype) for array in parameters],
                pltpu.SemaphoreType.DMA((8,)),
            ],
            compiler_params=pltpu.CompilerParams(
                collective_id=0, has_side_effects=True, vmem_limit_bytes=48 * 1024 * 1024
            ),
        )(frames, *parameters)
    )


def solution(mesh):
    return jax.shard_map(
        body,
        mesh=mesh,
        in_specs=(P(("groups", "dp"), ("tm", "state"), None), P(), P(), P(), P(), P(), P(), P()),
        out_specs=(
            P(("groups", "dp"), ("tm", "state"), None),
            P("groups", None, None),
            P("groups", None, None),
            P("groups", None),
            P("groups"),
        ),
        check_vma=False,
    )
```
